128 devices in a mesh: row: 8 (over x, core), col: 16 (over z, y).
Axes of the slice: x: 4, y: 4, z: 4, core: 2. Of those that a mesh axis runs over, the one named last changes fastest.
Arguments:
- sources: bfloat16 [64, 262144], P(None, 'row'), may hold values from -2 to 2
- targets: bfloat16 [64, 262144], P(None, 'col'), may hold values from -2 to 3, as said below
- log_a: float32 [262144], P('row'), may hold values from -6 to 0
- log_b: float32 [262144], P('col'), may hold values from -6 to 0
- block_cols: int32 [1024, 32], P('row', 'col'), may hold values from 0 to 63, as said below
- block_count: int32 [1024, 16], P('row', 'col'), may hold values from 0 to 2, as said below
Outputs:
- f_potential: float32 [262144], P('row')
- g_potential: float32 [262144], P('col')
The draws below stay inside these ranges and needn't reach their ends.
Inputs may be any that keep to these rules, and one draw needn't show every extreme that they name: `targets`: targets are real points; coordinates stay in the stated range. `block_cols`: slot numbers index column blocks of their own column shard; the used slots of one row block and shard name distinct blocks; slots at or beyond the count hold 0 and are ignored. Every column block is named by some row block. `block_count`: every row block uses at least one slot over all column shards.
All inputs are finite; a program needn't handle non-finite values.
Results may differ from the reference program's by a relative error of at most 0.0003.
Values sent between devices are 32-bit elements; how exact they have to be, the bound alone decides.
A program may use at most 64 MiB of HBM per device.

```python
import jax
import jax.numpy as jnp
from jax import lax

D = 64
BLOCK = 256
RB_DEV = 128
CB_DEV = 64
K = 2
ITERS = 2
NS = 262144
NT = 262144
N_COL = 16


def support_tables(key):
    nrb = NS // BLOCK
    ncol = NT // (BLOCK * CB_DEV)
    nrow = NS // (BLOCK * RB_DEV)
    keys = jax.random.split(key, 4)
    rolls = jax.random.randint(keys[0], (nrb, ncol), 0, 16)
    count = jnp.where(rolls < 3, 1, 0) + jnp.where(rolls == 3, 2, 0)
    count = jnp.minimum(count, K)
    rows = jnp.arange(nrb, dtype=jnp.int32)[:, None]
    shard = jnp.arange(ncol, dtype=jnp.int32)[None, :]
    forced = rows % ncol == shard
    count = jnp.where(forced, jnp.maximum(count, 1), count)
    hot_row = jax.random.randint(keys[1], (), 0, nrow)
    hot_col = jax.random.randint(keys[2], (), 0, ncol)
    hot = (rows // RB_DEV == hot_row) & (rows % RB_DEV % 4 == 0) & (shard == hot_col)
    count = jnp.where(hot, K, count)
    start = jax.random.randint(keys[3], (nrb, ncol), 0, CB_DEV)
    start = jnp.where(forced, rows // ncol % CB_DEV, start)
    slot = jnp.arange(K, dtype=jnp.int32)
    cols = (start[:, :, None] + slot[None, None, :]) % CB_DEV
    cols = jnp.where(slot[None, None, :] < count[:, :, None], cols, 0)
    return (cols.reshape(nrb, ncol * K).astype(jnp.int32), count.astype(jnp.int32))


def draw_block_cols(key, part):
    return support_tables(key)[0]


def draw_block_count(key, part):
    return support_tables(key)[1]


def draw_targets(key, part):
    key = jax.random.fold_in(key, 11)
    base = jnp.clip(jax.random.normal(key, (D, NT), jnp.float32) * 0.25, -2.0, 2.0)
    return base.astype(jnp.bfloat16)


def shard_levels(stream_key, shape, pieces, low, high):
    def one(position, blocks):
        heights = jax.random.uniform(jax.random.fold_in(jax.random.fold_in(stream_key, 6), position), (blocks,), jnp.float32, low / len(pieces), high / len(pieces))
        return jnp.repeat(jnp.exp(heights), shape[position] // blocks).reshape((-1,) + (1,) * (len(shape) - position - 1))

    level = one(*pieces[0])
    for cut in pieces[1:]:
        level = level * one(*cut)
    return level


def noise(rng, shape, scale, most, cuts=(), held_as=jnp.bfloat16):
    drawn = jax.random.normal(rng, shape, jnp.float32) * scale
    if len(cuts) > 0:
        drawn = shard_levels(rng, shape, cuts, -0.22, 0.18) * drawn
    return jnp.clip(drawn, min=-most, max=most).astype(held_as)


def setup_inputs(seed: int = 0) -> dict:
    key_list = jax.random.split(jax.random.key(seed), 7)
    return {
        "sources": noise(key_list[0], (D, NS), 0.25, 2.0, ((1, 8),)),
        "targets": draw_targets(jax.random.fold_in(key_list[6], 71), 0),
        "log_a": jnp.clip(-6.0 + 6.0 * jax.random.uniform(key_list[2], (NS,), jnp.float32) ** shard_levels(key_list[2], (NS,), ((0, 8),), -0.2, 0.2), -6.0, 0.0),
        "log_b": jnp.clip(-6.0 + 6.0 * jax.random.uniform(key_list[3], (NT,), jnp.float32) ** shard_levels(key_list[3], (NT,), ((0, 16),), -0.2, 0.2), -6.0, 0.0),
        "block_cols": draw_block_cols(jax.random.fold_in(key_list[6], 71), 0),
        "block_count": draw_block_count(jax.random.fold_in(key_list[6], 71), 0),
    }


EPS = 0.05
INV_EPS = 20.0
NEG = -1e30


def reference(sources, targets, log_a, log_b, block_cols, block_count):
    nrb = NS // BLOCK
    width = N_COL * K
    src = sources.astype(jnp.float32)
    tgt = targets.astype(jnp.float32)
    source_sq = 0.5 * jnp.sum(src * src, 0)
    target_sq = 0.5 * jnp.sum(tgt * tgt, 0)
    shard_base = (jnp.arange(N_COL, dtype=jnp.int32) * CB_DEV)[None, :, None]
    gblock = (shard_base + block_cols.reshape(nrb, N_COL, K)).reshape(nrb, width)
    live = (jnp.arange(K, dtype=jnp.int32)[None, None, :] < block_count[:, :, None]).reshape(nrb, width)
    inner = jnp.arange(BLOCK, dtype=jnp.int32)
    blocks = jnp.arange(nrb, dtype=jnp.int32)

    def costs(i):
        index = (gblock[i][:, None] * BLOCK + inner[None, :]).reshape(-1)
        xblock = lax.dynamic_slice_in_dim(sources, i * BLOCK, BLOCK, 1)
        yblock = jnp.take(targets, index, axis=1)
        inner_prod = lax.dot_general(xblock, yblock, (((0,), (0,)), ((), ())), preferred_element_type=jnp.float32)
        xnorm = lax.dynamic_slice_in_dim(source_sq, i * BLOCK, BLOCK)
        cost = xnorm[:, None] + target_sq[index][None, :] - inner_prod
        mask = jnp.repeat(live[i], BLOCK)
        return index, cost, mask

    def row_lse(g_pot):
        def one(i):
            index, cost, mask = costs(i)
            score = (g_pot[index][None, :] - cost) * INV_EPS
            score = jnp.where(mask[None, :], score, NEG)
            top = jnp.max(score, 1)
            total = jnp.sum(jnp.where(mask[None, :], jnp.exp(score - top[:, None]), 0.0), 1)
            return top + jnp.log(total)
        return lax.map(one, blocks).reshape(-1)

    def col_lse(f_pot):
        def top_step(carry, i):
            index, cost, mask = costs(i)
            fblock = lax.dynamic_slice_in_dim(f_pot, i * BLOCK, BLOCK)
            score = (fblock[:, None] - cost) * INV_EPS
            block_top = jnp.where(mask, jnp.max(score, 0), NEG)
            return carry.at[index].max(block_top), None

        top, _ = lax.scan(top_step, jnp.full((NT,), NEG, jnp.float32), blocks)

        def sum_step(carry, i):
            index, cost, mask = costs(i)
            fblock = lax.dynamic_slice_in_dim(f_pot, i * BLOCK, BLOCK)
            score = (fblock[:, None] - cost) * INV_EPS
            terms = jnp.where(mask[None, :], jnp.exp(score - top[index][None, :]), 0.0)
            return carry.at[index].add(jnp.sum(terms, 0)), None

        total, _ = lax.scan(sum_step, jnp.zeros((NT,), jnp.float32), blocks)
        return top + jnp.log(total)

    g_pot = jnp.zeros((NT,), jnp.float32)
    f_pot = jnp.zeros((NS,), jnp.float32)
    for step in range(ITERS):
        f_pot = EPS * (log_a - row_lse(g_pot))
        g_pot = EPS * (log_b - col_lse(f_pot))
    return f_pot, g_pot
```

```python
import functools

import jax
import jax.numpy as jnp
from jax import lax
from jax.experimental import pallas as pl
from jax.experimental.pallas import tpu as pltpu
from jax.sharding import PartitionSpec as P

BLOCK = 256
ITERS = 2
EPS = 0.05
LOG2_SCALE = 20.0 * 1.4426950408889634
NEG = -1e30
UNROLL = 4
AUG = 16
THRESHOLD = 2.0**-90
MESH = pl.DeviceIdType.MESH


def build_pairs(cols_ref, count_ref, pair_a, pair_b, npairs, row_blocks, slots):
    def add(b, n):
        used = count_ref[b]
        for s in range(slots):
            pair_a[n] = b
            pair_b[n] = cols_ref[b * slots + s]
            n = n + (s < used).astype(jnp.int32)
        return n

    total = lax.fori_loop(0, row_blocks, add, jnp.int32(0), unroll=4)
    for k in range(UNROLL):
        pair_a[total + k] = jnp.int32(-1)
        pair_b[total + k] = jnp.int32(-1)
    npairs[0] = total


def split3(v):
    hi = v.astype(jnp.bfloat16).astype(jnp.float32)
    rest = v - hi
    mid = rest.astype(jnp.bfloat16).astype(jnp.float32)
    return hi, mid, rest - mid


def half_norms(points_ref, out_ref, blocks):
    def one(b, carry):
        blk = points_ref[:, pl.ds(pl.multiple_of(b * BLOCK, BLOCK), BLOCK)].astype(jnp.float32)
        out_ref[pl.ds(b, 1), :] = 0.5 * jnp.sum(blk * blk, 0, keepdims=True)
        return carry

    lax.fori_loop(0, blocks, one, 0, unroll=4)


def pass_body(
    bias, red_ref, keep_ref, pot_red, pot_keep, pair_red, pair_keep, npairs_ref,
    rel_ref, red_parts, keep_parts, acc, top, touched,
):
    nred = pot_red.shape[0]
    nkeep = pot_keep.shape[0]
    npairs = npairs_ref[0]
    for part, value in enumerate(split3(pot_red[...])):
        red_parts[part] = value
    for part, value in enumerate(split3(pot_keep[...] + bias / LOG2_SCALE)):
        keep_parts[part] = value
    acc[...] = jnp.zeros_like(acc)
    touched[...] = jnp.zeros_like(touched)
    line = lax.broadcasted_iota(jnp.int32, (8, BLOCK), 0)
    zeros = jnp.zeros((8, BLOCK), jnp.float32)

    def rows(parts, index, first, ones):
        out = jnp.where((line >= ones) & (line < ones + 3), 1.0, 0.0)
        for part in range(3):
            out = jnp.where(line == first + part, parts[part, pl.ds(index, 1), :], out)
        return jnp.concatenate([out, zeros], 0).astype(jnp.bfloat16)

    def scores(p):
        slot_r = pair_red[p]
        slot_k = pair_keep[p]
        r = jnp.maximum(slot_r, 0)
        k = jnp.maximum(slot_k, 0)
        into = jnp.where(slot_k < 0, nkeep, slot_k)
        rblk = red_ref[:, pl.ds(pl.multiple_of(r * BLOCK, BLOCK), BLOCK)]
        kblk = keep_ref[:, pl.ds(pl.multiple_of(k * BLOCK, BLOCK), BLOCK)]
        lhs = jnp.concatenate([rblk, rows(red_parts, r, 0, 3)], 0)
        rhs = jnp.concatenate([kblk, rows(keep_parts, k, 3, 0)], 0)
        z = lax.dot_general(lhs, rhs, (((0,), (0,)), ((), ())), preferred_element_type=jnp.float32)
        return z, into

    def add_pair(p, shift):
        z, into = scores(p)
        if shift is not None:
            z = z - shift[pl.ds(into, 1), :]
        e = jnp.exp2(z * LOG2_SCALE)
        acc[into] += jnp.sum(e.reshape(BLOCK // 8, 8, BLOCK), 0)
        touched[pl.ds(into, 1), :] = jnp.ones((1, BLOCK), jnp.float32)

    def group(t, carry):
        for u in range(UNROLL):
            add_pair(t * UNROLL + u, None)
        return carry

    lax.fori_loop(0, (npairs + UNROLL - 1) // UNROLL, group, 0)
    total = jnp.sum(acc[:nkeep], 1)
    live = touched[:nkeep] > 0.0
    rel_ref[...] = jnp.where(live, jnp.log2(total) - bias, NEG)
    weak = jnp.max(jnp.where(live & (total < THRESHOLD), 1.0, 0.0))

    @pl.when(weak > 0.0)
    def _():
        acc[...] = jnp.full_like(acc, NEG)

        def top_pair(p, carry):
            z, into = scores(p)
            acc[into] = jnp.maximum(acc[into], jnp.max(z.reshape(BLOCK // 8, 8, BLOCK), 0))
            return carry

        lax.fori_loop(0, npairs, top_pair, 0)
        top[:nkeep] = jnp.max(acc[:nkeep], 1)
        acc[...] = jnp.zeros_like(acc)

        def sum_pair(p, carry):
            add_pair(p, top)
            return carry

        lax.fori_loop(0, npairs, sum_pair, 0)
        fixed = jnp.log2(jnp.sum(acc[:nkeep], 1)) + (top[:nkeep] * LOG2_SCALE - bias)
        rel_ref[...] = jnp.where(touched[:nkeep] > 0.0, fixed, NEG)


def first_kernel(
    bias, slots, sources, targets, cols, counts,
    rel, half_src, half_tgt, pair_row, pair_col, npairs,
    pot_src, pot_tgt, *scratch,
):
    build_pairs(cols, counts, pair_row, pair_col, npairs, half_src.shape[0], slots)
    half_norms(sources, half_src, half_src.shape[0])
    half_norms(targets, half_tgt, half_tgt.shape[0])
    pot_src[...] = -half_src[...]
    pot_tgt[...] = -half_tgt[...]
    pass_body(bias, targets, sources, pot_tgt, pot_src, pair_col, pair_row, npairs, rel, *scratch)


VMEM = pl.BlockSpec(memory_space=pltpu.VMEM)
SMEM = pl.BlockSpec(memory_space=pltpu.SMEM)


def pass_scratch(nred, nkeep):
    return [
        pltpu.VMEM((3, nred, BLOCK), jnp.float32),
        pltpu.VMEM((3, nkeep, BLOCK), jnp.float32),
        pltpu.VMEM((nkeep + 1, 8, BLOCK), jnp.float32),
        pltpu.VMEM((nkeep + 8, BLOCK), jnp.float32),
        pltpu.VMEM((nkeep + 8, BLOCK), jnp.float32),
    ]


def local_params():
    return pltpu.CompilerParams(vmem_limit_bytes=32 * 1024 * 1024)


def first_pass(bias, slots, nred, nkeep, sources, targets, cols, counts):
    most = nkeep * slots + UNROLL
    return pl.pallas_call(
        functools.partial(first_kernel, bias, slots),
        out_shape=(
            jax.ShapeDtypeStruct((nkeep, BLOCK), jnp.float32),
            jax.ShapeDtypeStruct((nkeep, BLOCK), jnp.float32),
            jax.ShapeDtypeStruct((nred, BLOCK), jnp.float32),
            jax.ShapeDtypeStruct((most,), jnp.int32),
            jax.ShapeDtypeStruct((most,), jnp.int32),
            jax.ShapeDtypeStruct((1,), jnp.int32),
        ),
        in_specs=[VMEM, VMEM, SMEM, SMEM],
        out_specs=(VMEM, VMEM, VMEM, SMEM, SMEM, SMEM),
        scratch_shapes=[
            pltpu.VMEM((nkeep, BLOCK), jnp.float32),
            pltpu.VMEM((nred, BLOCK), jnp.float32),
        ]
        + pass_scratch(nred, nkeep),
        compiler_params=local_params(),
        name="first_pass",
    )(sources, targets, cols, counts)


def later_pass(name, bias, red, keep, pot_red, pot_keep, pair_red, pair_keep, npairs):
    nred, nkeep = pot_red.shape[0], pot_keep.shape[0]
    return pl.pallas_call(
        functools.partial(pass_body, bias),
        out_shape=jax.ShapeDtypeStruct((nkeep, BLOCK), jnp.float32),
        in_specs=[VMEM, VMEM, VMEM, VMEM, SMEM, SMEM, SMEM],
        out_specs=VMEM,
        scratch_shapes=pass_scratch(nred, nkeep),
        compiler_params=local_params(),
        name=name,
    )(red, keep, pot_red, pot_keep, pair_red, pair_keep, npairs)


def exchange_kernel(axis, n, sign, rel, old, logw, out, landing, send1, recv1, send2, recv2):
    me = lax.axis_index(axis)
    chunk = rel.shape[0] // n
    mine = pl.ds(pl.multiple_of(me * chunk, 8), chunk)

    barrier = pltpu.get_barrier_semaphore()
    for k in range(1, n):
        pl.semaphore_signal(barrier, inc=1, device_id={axis: lax.rem(me + k, n)}, device_id_type=MESH)
    pl.semaphore_wait(barrier, n - 1)

    def scatter(k):
        peer = lax.rem(me + k, n)
        return pltpu.make_async_remote_copy(
            src_ref=rel.at[pl.ds(pl.multiple_of(peer * chunk, 8), chunk)],
            dst_ref=landing.at[k - 1],
            send_sem=send1.at[k - 1],
            recv_sem=recv1.at[k - 1],
            device_id={axis: peer},
            device_id_type=MESH,
        )

    def gather(k):
        peer = lax.rem(me + k, n)
        return pltpu.make_async_remote_copy(
            src_ref=out.at[mine],
            dst_ref=out.at[mine],
            send_sem=send2.at[k - 1],
            recv_sem=recv2.at[k - 1],
            device_id={axis: peer},
            device_id_type=MESH,
        )

    first = [scatter(k) for k in range(1, n)]
    for copy in first:
        copy.start()
    own = rel[mine]
    for copy in first:
        copy.wait_recv()
    top = jnp.maximum(own, jnp.max(landing[...], 0))
    total = jnp.exp2(own - top) + jnp.sum(jnp.exp2(landing[...] - top[None]), 0)
    lse = top + jnp.log2(total)
    out[mine] = sign * old[mine] + (EPS * logw[mine] - lse * (1.0 / LOG2_SCALE))
    second = [gather(k) for k in range(1, n)]
    for copy in second:
        copy.start()
    for copy in second:
        copy.wait_recv()
    for copy in first:
        copy.wait_send()
    for copy in second:
        copy.wait_send()


def exchange(axis, n, ident, sign, rel, old, logw):
    blocks = rel.shape[0]
    return pl.pallas_call(
        functools.partial(exchange_kernel, axis, n, sign),
        out_shape=jax.ShapeDtypeStruct((blocks, BLOCK), jnp.float32),
        in_specs=[VMEM] * 3,
        out_specs=VMEM,
        scratch_shapes=[pltpu.VMEM((n - 1, blocks // n, BLOCK), jnp.float32)]
        + [pltpu.SemaphoreType.DMA((n - 1,))] * 4,
        compiler_params=pltpu.CompilerParams(collective_id=ident, has_side_effects=True),
        name=f"exchange_{axis}_{ident}",
    )(rel, old, logw)


def per_device(nrow, ncol, sources, targets, log_a, log_b, block_cols, block_count):
    row_blocks, slots = block_cols.shape
    col_blocks = targets.shape[1] // BLOCK
    log_a = log_a.reshape(row_blocks, BLOCK)
    log_b = log_b.reshape(col_blocks, BLOCK)
    row_bias, col_bias = 112.0, 104.0

    rel, half_src, half_tgt, pair_row, pair_col, npairs = first_pass(
        row_bias, slots, col_blocks, row_blocks, sources, targets, block_cols.reshape(-1), block_count.reshape(-1)
    )
    f_pot, f_sign = half_src, -1.0
    g_pot = -half_tgt
    for step in range(ITERS):
        if step > 0:
            rel = later_pass("row_pass", row_bias, targets, sources, g_pot, f_pot, pair_col, pair_row, npairs)
        f_pot = exchange("col", ncol, 2 * step, f_sign, rel, f_pot, log_a)
        f_sign = 1.0
        rel = later_pass("col_pass", col_bias, sources, targets, f_pot, g_pot, pair_row, pair_col, npairs)
        g_pot = exchange("row", nrow, 2 * step + 1, 1.0, rel, g_pot, log_b)
    return ((f_pot + half_src).reshape(-1), (g_pot + half_tgt).reshape(-1))


def solution(mesh):
    return jax.shard_map(
        functools.partial(per_device, mesh.shape["row"], mesh.shape["col"]),
        mesh=mesh,
        in_specs=(
            P(None, "row"),
            P(None, "col"),
            P("row"),
            P("col"),
            P("row", "col"),
            P("row", "col"),
        ),
        out_specs=(P("row"), P("col")),
        check_vma=False,
    )
```

```python
import functools

import jax
import jax.numpy as jnp
from jax import lax
from jax.experimental import pallas as pl
from jax.experimental.pallas import tpu as pltpu
from jax.sharding import PartitionSpec as P

BLOCK = 256
LANES = 128
ITERS = 2
EPS = 0.05
LOG2_SCALE = 20.0 * 1.4426950408889634
NEG = -1e30
BIG_GROUP = 32
SMALL_GROUP = 8
PAD = 16
CHUNKS = 4
THRESHOLD = 2.0**-90
CEILING = 2.0**120
FIRST_BIAS = 40.0
ROW_BIAS = 112.0
COL_BIAS = 104.0
MESH = pl.DeviceIdType.MESH
MIB = 1024 * 1024


def build_pairs(cols_ref, count_ref, table, row_blocks, slots):
    row_at, col_at = table_starts(table)

    def add(b, n):
        used = count_ref[0, b]
        for s in range(slots):
            table[row_at + n] = b
            table[col_at + n] = cols_ref[s, b]
            n = n + (s < used).astype(jnp.int32)
        return n

    total = lax.fori_loop(0, row_blocks, add, jnp.int32(0), unroll=8)
    for k in range(PAD):
        table[row_at + total + k] = jnp.int32(-1)
        table[col_at + total + k] = jnp.int32(-1)
    table[0] = total


def table_starts(table):
    return 8, 8 + (table.shape[0] - 8) // 2


def split3(v):
    hi = v.astype(jnp.bfloat16).astype(jnp.float32)
    rest = v - hi
    mid = rest.astype(jnp.bfloat16).astype(jnp.float32)
    return hi, mid, rest - mid


def half_norms(points, first, out_ref, start, stop):
    def one(b, carry):
        blk = points[:, pl.ds(pl.multiple_of((first + b) * BLOCK, BLOCK), BLOCK)].astype(jnp.float32)
        norm = 0.5 * jnp.sum(blk * blk, 0, keepdims=True)
        out_ref[pl.ds(2 * b, 1), :] = norm[:, :LANES]
        out_ref[pl.ds(2 * b + 1, 1), :] = norm[:, LANES:]
        return carry

    lax.fori_loop(start, stop, one, 0, unroll=4)


def lse_pass(
    bias, by_row, points, pot_red, pot_keep, table,
    rel_ref, red_parts, keep_parts, acc, top, touched,
):
    nkeep = rel_ref.shape[0] // 2
    npairs = table[0]
    keep_at, red_at = table_starts(table) if by_row else table_starts(table)[::-1]
    nred = pot_red.shape[0] // 2
    red_first, keep_first = (nkeep, 0) if by_row else (0, nred)
    shift = bias / LOG2_SCALE
    for part, value in enumerate(split3(pot_red[...])):
        red_parts[part] = value
    kept = pot_keep[...] + shift if pot_keep is not None else jnp.full(rel_ref.shape, shift, jnp.float32)
    for part, value in enumerate(split3(kept)):
        keep_parts[part] = value
    acc[...] = jnp.zeros_like(acc)
    touched[...] = jnp.zeros_like(touched)
    line = lax.broadcasted_iota(jnp.int32, (8, LANES), 0)
    zeros = jnp.zeros((8, LANES), jnp.float32)

    def rows(parts, index, first, ones):
        halves = []
        for half in range(2):
            out = jnp.where((line >= ones) & (line < ones + 3), 1.0, 0.0)
            for part in range(3):
                out = jnp.where(line == first + part, parts[part, pl.ds(2 * index + half, 1), :], out)
            halves.append(jnp.concatenate([out, zeros], 0).astype(jnp.bfloat16))
        return jnp.concatenate(halves, 1)

    def scores(p):
        slot_r = table[red_at + p]
        slot_k = table[keep_at + p]
        r = jnp.maximum(slot_r, 0)
        k = jnp.maximum(slot_k, 0)
        into = jnp.where(slot_k < 0, nkeep, slot_k)
        rblk = points[:, pl.ds(pl.multiple_of((red_first + r) * BLOCK, BLOCK), BLOCK)]
        kblk = points[:, pl.ds(pl.multiple_of((keep_first + k) * BLOCK, BLOCK), BLOCK)]
        lhs = jnp.concatenate([rblk, rows(red_parts, r, 0, 3)], 0)
        rhs = jnp.concatenate([kblk, rows(keep_parts, k, 3, 0)], 0)
        z = lax.dot_general(lhs, rhs, (((0,), (0,)), ((), ())), preferred_element_type=jnp.float32)
        return z, into

    def add_pair(p, shifted):
        z, into = scores(p)
        if shifted:
            z = z - jnp.concatenate([top[pl.ds(2 * into + half, 1), :] for half in range(2)], 1)
        part = jnp.sum(jnp.exp2(z * LOG2_SCALE), 0, keepdims=True)
        acc[pl.ds(2 * into, 1), :] += part[:, :LANES]
        acc[pl.ds(2 * into + 1, 1), :] += part[:, LANES:]
        touched[pl.ds(2 * into, 2), :] = jnp.ones((2, LANES), jnp.float32)

    def groups(size, base, trips):
        def group(t, carry):
            for u in range(size):
                add_pair(base + t * size + u, False)
            return carry

        lax.fori_loop(0, trips, group, 0)

    whole = (npairs + PAD - 1) // BIG_GROUP
    left = jnp.maximum(npairs - whole * BIG_GROUP, 0)
    groups(BIG_GROUP, 0, whole)
    groups(SMALL_GROUP, whole * BIG_GROUP, (left + SMALL_GROUP - 1) // SMALL_GROUP)
    total = acc[: 2 * nkeep]
    live = touched[: 2 * nkeep] > 0.0
    rel_ref[...] = jnp.where(live, jnp.log2(total) - bias, NEG)
    fine = (total >= THRESHOLD) & (total <= CEILING)
    weak = jnp.max(jnp.where(live & ~fine, 1.0, 0.0))

    @pl.when(weak > 0.0)
    def _():
        top[...] = jnp.full_like(top, NEG)

        def top_pair(p, carry):
            z, into = scores(p)
            part = jnp.max(z, 0, keepdims=True)
            for half in range(2):
                at = pl.ds(2 * into + half, 1)
                top[at, :] = jnp.maximum(top[at, :], part[:, half * LANES : (half + 1) * LANES])
            return carry

        lax.fori_loop(0, npairs, top_pair, 0)
        acc[...] = jnp.zeros_like(acc)

        def sum_pair(p, carry):
            add_pair(p, True)
            return carry

        lax.fori_loop(0, npairs, sum_pair, 0)
        fixed = jnp.log2(acc[: 2 * nkeep]) + (top[: 2 * nkeep] * LOG2_SCALE - bias)
        rel_ref[...] = jnp.where(touched[: 2 * nkeep] > 0.0, fixed, NEG)


def first_kernel(
    slots, sources, targets, cols, counts,
    rel, points, half_tgt, table,
    pot_tgt, cols_here, counts_here, sem_src, sem_tgt, sem_list, *scratch,
):
    row_blocks = rel.shape[0] // 2
    col_blocks = half_tgt.shape[0] // 2

    def chunk(whole, first, sem, c):
        width = whole.shape[1] // CHUNKS
        into = pl.ds(first * BLOCK + c * width, width)
        return pltpu.make_async_copy(whole.at[:, pl.ds(c * width, width)], points.at[:, into], sem.at[c])

    list_copies = [
        pltpu.make_async_copy(cols, cols_here, sem_list.at[0]),
        pltpu.make_async_copy(counts, counts_here, sem_list.at[1]),
    ]
    tgt_copies = [chunk(targets, row_blocks, sem_tgt, c) for c in range(CHUNKS)]
    src_copies = [chunk(sources, 0, sem_src, c) for c in range(CHUNKS)]
    for copy in list_copies + tgt_copies + src_copies:
        copy.start()
    for copy in list_copies:
        copy.wait()
    build_pairs(cols_here, counts_here, table, row_blocks, slots)
    for c, copy in enumerate(tgt_copies):
        copy.wait()
        half_norms(points, row_blocks, half_tgt, c * col_blocks // CHUNKS, (c + 1) * col_blocks // CHUNKS)
    pot_tgt[...] = -half_tgt[...]
    for copy in src_copies:
        copy.wait()
    lse_pass(FIRST_BIAS, True, points, pot_tgt, None, table, rel, *scratch)


def last_kernel(bias, points, f_pot, g_pot, half_src, table, rel, f_final, f_here, sem, *scratch):
    f_here[...] = f_pot[...] + half_src[...]
    copy = pltpu.make_async_copy(f_here, f_final, sem)
    copy.start()
    lse_pass(bias, False, points, f_pot, g_pot, table, rel, *scratch)
    copy.wait()


VMEM = pl.BlockSpec(memory_space=pltpu.VMEM)
SMEM = pl.BlockSpec(memory_space=pltpu.SMEM)
HBM = pl.BlockSpec(memory_space=pltpu.HBM)
ANY = pl.BlockSpec(memory_space=pl.ANY)


def pass_scratch(nred, nkeep):
    return [
        pltpu.VMEM((3, 2 * nred, LANES), jnp.float32),
        pltpu.VMEM((3, 2 * nkeep, LANES), jnp.float32),
        pltpu.VMEM((2 * nkeep + 8, LANES), jnp.float32),
        pltpu.VMEM((2 * nkeep + 8, LANES), jnp.float32),
        pltpu.VMEM((2 * nkeep + 8, LANES), jnp.float32),
    ]


def potential(blocks):
    return jax.ShapeDtypeStruct((2 * blocks, LANES), jnp.float32)


def first_pass(sources, targets, cols, counts):
    slots = cols.shape[0]
    nkeep = sources.shape[1] // BLOCK
    nred = targets.shape[1] // BLOCK
    return pl.pallas_call(
        functools.partial(first_kernel, slots),
        out_shape=(
            potential(nkeep),
            jax.ShapeDtypeStruct((sources.shape[0], sources.shape[1] + targets.shape[1]), sources.dtype),
            potential(nred),
            jax.ShapeDtypeStruct((8 + 2 * (nkeep * slots + PAD),), jnp.int32),
        ),
        in_specs=[HBM, HBM, HBM, HBM],
        out_specs=(VMEM, VMEM, VMEM, SMEM),
        scratch_shapes=[
            pltpu.VMEM((2 * nred, LANES), jnp.float32),
            pltpu.SMEM(cols.shape, jnp.int32),
            pltpu.SMEM(counts.shape, jnp.int32),
            pltpu.SemaphoreType.DMA((CHUNKS,)),
            pltpu.SemaphoreType.DMA((CHUNKS,)),
            pltpu.SemaphoreType.DMA((2,)),
        ]
        + pass_scratch(nred, nkeep),
        compiler_params=pltpu.CompilerParams(vmem_limit_bytes=24 * MIB),
        name="first_pass",
    )(*(pltpu.with_memory_space_constraint(a, pltpu.HBM) for a in (sources, targets, cols, counts)))


def later_pass(name, bias, by_row, points, pot_red, pot_keep, table, norms=None):
    nred, nkeep = pot_red.shape[0] // 2, pot_keep.shape[0] // 2
    params = pltpu.CompilerParams(vmem_limit_bytes=16 * MIB)
    if norms is None:
        return pl.pallas_call(
            functools.partial(lse_pass, bias, by_row),
            out_shape=potential(nkeep),
            in_specs=[VMEM] * 3 + [SMEM],
            out_specs=VMEM,
            scratch_shapes=pass_scratch(nred, nkeep),
            compiler_params=params,
            name=name,
        )(points, pot_red, pot_keep, table)
    return pl.pallas_call(
        functools.partial(last_kernel, bias),
        out_shape=(potential(nkeep), potential(nred)),
        in_specs=[VMEM] * 4 + [SMEM],
        out_specs=(VMEM, HBM),
        scratch_shapes=[pltpu.VMEM((2 * nred, LANES), jnp.float32), pltpu.SemaphoreType.DMA]
        + pass_scratch(nred, nkeep),
        compiler_params=params,
        name=name,
    )(points, pot_red, pot_keep, norms, table)


def offsets(outer, inner):
    def far(step):
        return min(step[0], outer - step[0]) + min(step[1], inner - step[1])

    steps = [(a, b) for a in range(outer) for b in range(inner) if a or b]
    return sorted(steps, key=lambda step: -far(step))


def exchange_kernel(axis, sides, has_old, with_norms, *refs):
    refs = list(refs)
    rel = refs.pop(0)
    old = refs.pop(0) if has_old else None
    logw = refs.pop(0)
    points = refs.pop(0) if with_norms else None
    out = refs.pop(0)
    norms = refs.pop(0) if with_norms else None
    landing, weights, wsem, send1, recv1, send2, recv2 = refs
    outer, inner = sides
    n = outer * inner
    steps = offsets(outer, inner)
    me = lax.axis_index(axis)
    peers = [
        lax.rem(me // inner + a, outer) * inner + lax.rem(lax.rem(me, inner) + b, inner) for a, b in steps
    ]
    chunk = rel.shape[0] // n
    mine = pl.ds(pl.multiple_of(me * chunk, 8), chunk)
    fetch = pltpu.make_async_copy(logw.at[mine], weights, wsem)
    fetch.start()

    barrier = pltpu.get_barrier_semaphore()
    for peer in peers:
        pl.semaphore_signal(barrier, inc=1, device_id={axis: peer}, device_id_type=MESH)
    pl.semaphore_wait(barrier, n - 1)

    def scatter(k):
        peer = peers[k]
        return pltpu.make_async_remote_copy(
            src_ref=rel.at[pl.ds(pl.multiple_of(peer * chunk, 8), chunk)],
            dst_ref=landing.at[k],
            send_sem=send1.at[k],
            recv_sem=recv1.at[k],
            device_id={axis: peer},
            device_id_type=MESH,
        )

    def gather(k):
        peer = peers[k]
        return pltpu.make_async_remote_copy(
            src_ref=out.at[mine],
            dst_ref=out.at[mine],
            send_sem=send2.at[k],
            recv_sem=recv2.at[k],
            device_id={axis: peer},
            device_id_type=MESH,
        )

    first = [scatter(k) for k in range(n - 1)]
    for copy in first:
        copy.start()
    if with_norms:
        half_norms(points, 0, norms, 0, rel.shape[0] // 2)
    own = rel[mine]
    fetch.wait()
    base = EPS * weights[...]
    if has_old:
        base = base + old[mine]
    for copy in first:
        copy.wait_recv()
    top = jnp.maximum(own, jnp.max(landing[...], 0))
    total = jnp.exp2(own - top) + jnp.sum(jnp.exp2(landing[...] - top[None]), 0)
    out[mine] = base - (top + jnp.log2(total)) * (1.0 / LOG2_SCALE)
    second = [gather(k) for k in range(n - 1)]
    for copy in second:
        copy.start()
    for copy in second:
        copy.wait_recv()
    for copy in first:
        copy.wait_send()
    for copy in second:
        copy.wait_send()


def exchange(axis, sides, ident, rel, old, logw, points=None):
    lines = rel.shape[0]
    n = sides[0] * sides[1]
    shape = jax.ShapeDtypeStruct((lines, LANES), jnp.float32)
    has_old, with_norms = old is not None, points is not None
    args = [rel] + ([old] if has_old else []) + [logw] + ([points] if with_norms else [])
    specs = [VMEM] + ([VMEM] if has_old else []) + [ANY] + ([VMEM] if with_norms else [])
    return pl.pallas_call(
        functools.partial(exchange_kernel, axis, sides, has_old, with_norms),
        out_shape=(shape, shape) if with_norms else shape,
        in_specs=specs,
        out_specs=(VMEM, VMEM) if with_norms else VMEM,
        scratch_shapes=[
            pltpu.VMEM((n - 1, lines // n, LANES), jnp.float32),
            pltpu.VMEM((lines // n, LANES), jnp.float32),
            pltpu.SemaphoreType.DMA,
        ]
        + [pltpu.SemaphoreType.DMA((n - 1,))] * 4,
        compiler_params=pltpu.CompilerParams(
            collective_id=ident, has_side_effects=True, vmem_limit_bytes=(12 if with_norms else 4) * MIB
        ),
        name=f"exchange_{axis}_{ident}",
    )(*args)


def sides_of(n):
    return (4, n // 4) if n % 4 == 0 else (n, 1)


def per_device(nrow, ncol, sources, targets, log_a, log_b, block_cols, block_count):
    row_sides, col_sides = sides_of(nrow), sides_of(ncol)
    log_a = log_a.reshape(-1, LANES)
    log_b = log_b.reshape(-1, LANES)
    rel, points, half_tgt, table = first_pass(sources, targets, block_cols.T, block_count.T)
    g_pot = -half_tgt
    f_pot = half_src = f_out = None
    for step in range(ITERS):
        if step > 0:
            rel = later_pass("row_pass", ROW_BIAS, True, points, g_pot, f_pot, table)
            f_pot = exchange("col", col_sides, 2 * step, rel, f_pot, log_a)
        else:
            f_pot, half_src = exchange("col", col_sides, 2 * step, rel, None, log_a, points)
        if step < ITERS - 1:
            rel = later_pass("col_pass", COL_BIAS, False, points, f_pot, g_pot, table)
        else:
            rel, f_out = later_pass("last_pass", COL_BIAS, False, points, f_pot, g_pot, table, half_src)
        g_pot = exchange("row", row_sides, 2 * step + 1, rel, g_pot, log_b)
    return (f_out.reshape(-1), (g_pot + half_tgt).reshape(-1))


def solution(mesh):
    return jax.shard_map(
        functools.partial(per_device, mesh.shape["row"], mesh.shape["col"]),
        mesh=mesh,
        in_specs=(
            P(None, "row"),
            P(None, "col"),
            P("row"),
            P("col"),
            P("row", "col"),
            P("row", "col"),
        ),
        out_specs=(P("row"), P("col")),
        check_vma=False,
    )
```

```python
import functools

import jax
import jax.numpy as jnp
from jax import lax
from jax.experimental import pallas as pl
from jax.experimental.pallas import tpu as pltpu
from jax.sharding import PartitionSpec as P

BLOCK = 256
LANES = 128
ITERS = 2
EPS = 0.05
LOG2_SCALE = 20.0 * 1.4426950408889634
NEG = -1e30
BIG_GROUP = 48
FIRST_GROUP = 24
SMALL_GROUP = 8
PAD = 16
CHUNKS = 4
SOURCE_CHUNKS = 8
ROW_SHIFT = 16
THRESHOLD = 2.0**-90
CEILING = 2.0**120
FIRST_BIAS = 40.0
ROW_BIAS = 112.0
COL_BIAS = 104.0
MESH = pl.DeviceIdType.MESH
MIB = 1024 * 1024


TABLE_START = 8


def add_pairs(cols_ref, count_ref, table, b, n, slots):
    for s in range(slots):
        table[TABLE_START + n + s] = (b << ROW_SHIFT) + cols_ref[s, b]
    return n + count_ref[0, b]


def close_table(table, total):
    for k in range(PAD):
        table[TABLE_START + total + k] = jnp.int32(-1)
    table[0] = total


def split3(v):
    hi = v.astype(jnp.bfloat16).astype(jnp.float32)
    rest = v - hi
    mid = rest.astype(jnp.bfloat16).astype(jnp.float32)
    return hi, mid, rest - mid


def half_norm(points, first, out_ref, b):
    blk = points[:, pl.ds(pl.multiple_of((first + b) * BLOCK, BLOCK), BLOCK)].astype(jnp.float32)
    norm = 0.5 * jnp.sum(blk * blk, 0, keepdims=True)
    out_ref[pl.ds(2 * b, 1), :] = norm[:, :LANES]
    out_ref[pl.ds(2 * b + 1, 1), :] = norm[:, LANES:]


def half_norms(points, first, out_ref, blocks):
    def one(b, carry):
        half_norm(points, first, out_ref, b)
        return carry

    lax.fori_loop(0, blocks, one, 0, unroll=4)


def lse_pass(
    bias, by_row, points, pot_red, pot_keep, table,
    rel_ref, red_parts, keep_parts, acc, top, touched, big=BIG_GROUP, arrive=None,
):
    nkeep = rel_ref.shape[0] // 2
    npairs = table[0]
    nred = pot_red.shape[0] // 2
    red_first, keep_first = (nkeep, 0) if by_row else (0, nred)
    shift = bias / LOG2_SCALE
    for part, value in enumerate(split3(pot_red[...])):
        red_parts[part] = value
    kept = pot_keep[...] + shift if pot_keep is not None else jnp.full(rel_ref.shape, shift, jnp.float32)
    for part, value in enumerate(split3(kept)):
        keep_parts[part] = value
    acc[...] = jnp.zeros_like(acc)
    touched[...] = jnp.zeros_like(touched)
    line = lax.broadcasted_iota(jnp.int32, (8, LANES), 0)
    zeros = jnp.zeros((8, LANES), jnp.float32)

    def rows(parts, index, first, ones):
        halves = []
        for half in range(2):
            out = jnp.where((line >= ones) & (line < ones + 3), 1.0, 0.0)
            for part in range(3):
                out = jnp.where(line == first + part, parts[part, pl.ds(2 * index + half, 1), :], out)
            halves.append(jnp.concatenate([out, zeros], 0).astype(jnp.bfloat16))
        return jnp.concatenate(halves, 1)

    def scores(p):
        word = table[TABLE_START + p]
        pair = jnp.maximum(word, 0)
        row, col = pair >> ROW_SHIFT, pair & ((1 << ROW_SHIFT) - 1)
        k, r = (row, col) if by_row else (col, row)
        into = jnp.where(word < 0, nkeep, k)
        rblk = points[:, pl.ds(pl.multiple_of((red_first + r) * BLOCK, BLOCK), BLOCK)]
        kblk = points[:, pl.ds(pl.multiple_of((keep_first + k) * BLOCK, BLOCK), BLOCK)]
        lhs = jnp.concatenate([rblk, rows(red_parts, r, 0, 3)], 0)
        rhs = jnp.concatenate([kblk, rows(keep_parts, k, 3, 0)], 0)
        z = lax.dot_general(lhs, rhs, (((0,), (0,)), ((), ())), preferred_element_type=jnp.float32)
        return z, into

    def add_pair(p, shifted):
        z, into = scores(p)
        if shifted:
            z = z - jnp.concatenate([top[pl.ds(2 * into + half, 1), :] for half in range(2)], 1)
        part = jnp.sum(jnp.exp2(z * LOG2_SCALE), 0, keepdims=True)
        acc[pl.ds(2 * into, 1), :] += part[:, :LANES]
        acc[pl.ds(2 * into + 1, 1), :] += part[:, LANES:]
        touched[pl.ds(2 * into, 2), :] = jnp.ones((2, LANES), jnp.float32)

    def groups(size, base, trips, here):
        def group(t, here):
            first = base + t * size
            if arrive is not None:
                last = table[TABLE_START + jnp.minimum(first + size, npairs) - 1]
                here = arrive(here, last >> ROW_SHIFT)
            for u in range(size):
                add_pair(first + u, False)
            return here

        return lax.fori_loop(0, trips, group, here)

    whole = (npairs + PAD - 1) // big
    left = jnp.maximum(npairs - whole * big, 0)
    here = groups(big, 0, whole, jnp.int32(0))
    here = groups(SMALL_GROUP, whole * big, (left + SMALL_GROUP - 1) // SMALL_GROUP, here)
    if arrive is not None:
        arrive(here, None)
    total = acc[: 2 * nkeep]
    live = touched[: 2 * nkeep] > 0.0
    rel_ref[...] = jnp.where(live, jnp.log2(total) - bias, NEG)
    fine = (total >= THRESHOLD) & (total <= CEILING)
    weak = jnp.max(jnp.where(live & ~fine, 1.0, 0.0))

    @pl.when(weak > 0.0)
    def _():
        top[...] = jnp.full_like(top, NEG)

        def top_pair(p, carry):
            z, into = scores(p)
            part = jnp.max(z, 0, keepdims=True)
            for half in range(2):
                at = pl.ds(2 * into + half, 1)
                top[at, :] = jnp.maximum(top[at, :], part[:, half * LANES : (half + 1) * LANES])
            return carry

        lax.fori_loop(0, npairs, top_pair, 0)
        acc[...] = jnp.zeros_like(acc)

        def sum_pair(p, carry):
            add_pair(p, True)
            return carry

        lax.fori_loop(0, npairs, sum_pair, 0)
        fixed = jnp.log2(acc[: 2 * nkeep]) + (top[: 2 * nkeep] * LOG2_SCALE - bias)
        rel_ref[...] = jnp.where(touched[: 2 * nkeep] > 0.0, fixed, NEG)


def first_kernel(
    slots, sources, targets, cols, counts,
    rel, points, half_tgt, table,
    pot_tgt, cols_here, counts_here, sem_src, sem_tgt, sem_list, *scratch,
):
    row_blocks = rel.shape[0] // 2
    col_blocks = half_tgt.shape[0] // 2

    def chunk(whole, first, sem, chunks, c):
        width = whole.shape[1] // chunks
        start = c * width if isinstance(c, int) else pl.multiple_of(c * width, LANES)
        into = pl.ds(first * BLOCK + start, width)
        return pltpu.make_async_copy(whole.at[:, pl.ds(start, width)], points.at[:, into], sem.at[c])

    list_copies = [
        pltpu.make_async_copy(cols, cols_here, sem_list.at[0]),
        pltpu.make_async_copy(counts, counts_here, sem_list.at[1]),
    ]
    tgt_copies = [chunk(targets, row_blocks, sem_tgt, CHUNKS, c) for c in range(CHUNKS)]
    src_copies = [chunk(sources, 0, sem_src, SOURCE_CHUNKS, c) for c in range(SOURCE_CHUNKS)]
    ahead = SOURCE_CHUNKS // CHUNKS
    for copy in list_copies + tgt_copies + src_copies[:ahead]:
        copy.start()
    for copy in list_copies:
        copy.wait()

    parts = col_blocks // 4
    per_part = row_blocks // parts

    def prepare(t, n):
        for u in range(4):
            half_norm(points, row_blocks, half_tgt, 4 * t + u)
        for u in range(per_part):
            n = add_pairs(cols_here, counts_here, table, per_part * t + u, n, slots)
        return n

    total = jnp.int32(0)
    for c, copy in enumerate(tgt_copies):
        copy.wait()
        for later in src_copies[(c + 1) * ahead : (c + 2) * ahead]:
            later.start()
        total = lax.fori_loop(c * parts // CHUNKS, (c + 1) * parts // CHUNKS, prepare, total)
    close_table(table, total)
    pot_tgt[...] = -half_tgt[...]

    def arrive(here, row):
        stop = SOURCE_CHUNKS if row is None else row // (row_blocks // SOURCE_CHUNKS) + 1

        def one(c, carry):
            chunk(sources, 0, sem_src, SOURCE_CHUNKS, c).wait()
            return carry

        lax.fori_loop(here, stop, one, 0)
        return jnp.maximum(here, stop)

    lse_pass(FIRST_BIAS, True, points, pot_tgt, None, table, rel, *scratch, big=FIRST_GROUP, arrive=arrive)


def last_kernel(bias, points, f_pot, g_pot, half_src, table, rel, f_final, f_here, sem, *scratch):
    f_here[...] = f_pot[...] + half_src[...]
    copy = pltpu.make_async_copy(f_here, f_final, sem)
    copy.start()
    lse_pass(bias, False, points, f_pot, g_pot, table, rel, *scratch)
    copy.wait()


VMEM = pl.BlockSpec(memory_space=pltpu.VMEM)
SMEM = pl.BlockSpec(memory_space=pltpu.SMEM)
HBM = pl.BlockSpec(memory_space=pltpu.HBM)
ANY = pl.BlockSpec(memory_space=pl.ANY)


def pass_scratch(nred, nkeep):
    return [
        pltpu.VMEM((3, 2 * nred, LANES), jnp.float32),
        pltpu.VMEM((3, 2 * nkeep, LANES), jnp.float32),
        pltpu.VMEM((2 * nkeep + 8, LANES), jnp.float32),
        pltpu.VMEM((2 * nkeep + 8, LANES), jnp.float32),
        pltpu.VMEM((2 * nkeep + 8, LANES), jnp.float32),
    ]


def potential(blocks):
    return jax.ShapeDtypeStruct((2 * blocks, LANES), jnp.float32)


def first_pass(sources, targets, cols, counts):
    slots = cols.shape[0]
    nkeep = sources.shape[1] // BLOCK
    nred = targets.shape[1] // BLOCK
    return pl.pallas_call(
        functools.partial(first_kernel, slots),
        out_shape=(
            potential(nkeep),
            jax.ShapeDtypeStruct((sources.shape[0], sources.shape[1] + targets.shape[1]), sources.dtype),
            potential(nred),
            jax.ShapeDtypeStruct((TABLE_START + nkeep * slots + PAD,), jnp.int32),
        ),
        in_specs=[HBM, HBM, HBM, HBM],
        out_specs=(VMEM, VMEM, VMEM, SMEM),
        scratch_shapes=[
            pltpu.VMEM((2 * nred, LANES), jnp.float32),
            pltpu.SMEM(cols.shape, jnp.int32),
            pltpu.SMEM(counts.shape, jnp.int32),
            pltpu.SemaphoreType.DMA((SOURCE_CHUNKS,)),
            pltpu.SemaphoreType.DMA((CHUNKS,)),
            pltpu.SemaphoreType.DMA((2,)),
        ]
        + pass_scratch(nred, nkeep),
        compiler_params=pltpu.CompilerParams(vmem_limit_bytes=24 * MIB),
        name="first_pass",
    )(*(pltpu.with_memory_space_constraint(a, pltpu.HBM) for a in (sources, targets, cols, counts)))


def later_pass(name, bias, by_row, points, pot_red, pot_keep, table, norms=None):
    nred, nkeep = pot_red.shape[0] // 2, pot_keep.shape[0] // 2
    params = pltpu.CompilerParams(vmem_limit_bytes=16 * MIB)
    if norms is None:
        return pl.pallas_call(
            functools.partial(lse_pass, bias, by_row),
            out_shape=potential(nkeep),
            in_specs=[VMEM] * 3 + [SMEM],
            out_specs=VMEM,
            scratch_shapes=pass_scratch(nred, nkeep),
            compiler_params=params,
            name=name,
        )(points, pot_red, pot_keep, table)
    return pl.pallas_call(
        functools.partial(last_kernel, bias),
        out_shape=(potential(nkeep), potential(nred)),
        in_specs=[VMEM] * 4 + [SMEM],
        out_specs=(VMEM, HBM),
        scratch_shapes=[pltpu.VMEM((2 * nred, LANES), jnp.float32), pltpu.SemaphoreType.DMA]
        + pass_scratch(nred, nkeep),
        compiler_params=params,
        name=name,
    )(points, pot_red, pot_keep, norms, table)


def offsets(outer, inner):
    def far(step):
        return min(step[0], outer - step[0]) + min(step[1], inner - step[1])

    steps = [(a, b) for a in range(outer) for b in range(inner) if a or b]
    return sorted(steps, key=lambda step: -far(step))


def exchange_kernel(axis, sides, has_old, with_norms, *refs):
    refs = list(refs)
    rel = refs.pop(0)
    old = refs.pop(0) if has_old else None
    logw = refs.pop(0)
    points = refs.pop(0) if with_norms else None
    out = refs.pop(0)
    norms = refs.pop(0) if with_norms else None
    landing, weights, wsem, send1, recv1, send2, recv2 = refs
    outer, inner = sides
    n = outer * inner
    steps = offsets(outer, inner)
    me = lax.axis_index(axis)
    peers = [
        lax.rem(me // inner + a, outer) * inner + lax.rem(lax.rem(me, inner) + b, inner) for a, b in steps
    ]
    chunk = rel.shape[0] // n
    mine = pl.ds(pl.multiple_of(me * chunk, 8), chunk)
    fetch = pltpu.make_async_copy(logw.at[mine], weights, wsem)
    fetch.start()

    barrier = pltpu.get_barrier_semaphore()
    for peer in peers:
        pl.semaphore_signal(barrier, inc=1, device_id={axis: peer}, device_id_type=MESH)
    pl.semaphore_wait(barrier, n - 1)

    def scatter(k):
        peer = peers[k]
        return pltpu.make_async_remote_copy(
            src_ref=rel.at[pl.ds(pl.multiple_of(peer * chunk, 8), chunk)],
            dst_ref=landing.at[k],
            send_sem=send1.at[k],
            recv_sem=recv1.at[k],
            device_id={axis: peer},
            device_id_type=MESH,
        )

    def gather(k):
        peer = peers[k]
        return pltpu.make_async_remote_copy(
            src_ref=out.at[mine],
            dst_ref=out.at[mine],
            send_sem=send2.at[k],
            recv_sem=recv2.at[k],
            device_id={axis: peer},
            device_id_type=MESH,
        )

    first = [scatter(k) for k in range(n - 1)]
    for copy in first:
        copy.start()
    if with_norms:
        half_norms(points, 0, norms, rel.shape[0] // 2)
    own = rel[mine]
    fetch.wait()
    base = EPS * weights[...]
    if has_old:
        base = base + old[mine]
    for copy in first:
        copy.wait_recv()
    top = jnp.maximum(own, jnp.max(landing[...], 0))
    total = jnp.exp2(own - top) + jnp.sum(jnp.exp2(landing[...] - top[None]), 0)
    out[mine] = base - (top + jnp.log2(total)) * (1.0 / LOG2_SCALE)
    second = [gather(k) for k in range(n - 1)]
    for copy in second:
        copy.start()
    for copy in second:
        copy.wait_recv()
    for copy in first:
        copy.wait_send()
    for copy in second:
        copy.wait_send()


def exchange(axis, sides, ident, rel, old, logw, points=None):
    lines = rel.shape[0]
    n = sides[0] * sides[1]
    shape = jax.ShapeDtypeStruct((lines, LANES), jnp.float32)
    has_old, with_norms = old is not None, points is not None
    args = [rel] + ([old] if has_old else []) + [logw] + ([points] if with_norms else [])
    specs = [VMEM] + ([VMEM] if has_old else []) + [ANY] + ([VMEM] if with_norms else [])
    return pl.pallas_call(
        functools.partial(exchange_kernel, axis, sides, has_old, with_norms),
        out_shape=(shape, shape) if with_norms else shape,
        in_specs=specs,
        out_specs=(VMEM, VMEM) if with_norms else VMEM,
        scratch_shapes=[
            pltpu.VMEM((n - 1, lines // n, LANES), jnp.float32),
            pltpu.VMEM((lines // n, LANES), jnp.float32),
            pltpu.SemaphoreType.DMA,
        ]
        + [pltpu.SemaphoreType.DMA((n - 1,))] * 4,
        compiler_params=pltpu.CompilerParams(
            collective_id=ident, has_side_effects=True, vmem_limit_bytes=(12 if with_norms else 4) * MIB
        ),
        name=f"exchange_{axis}_{ident}",
    )(*args)


def sides_of(n):
    return (4, n // 4) if n % 4 == 0 else (n, 1)


def per_device(nrow, ncol, sources, targets, log_a, log_b, block_cols, block_count):
    row_sides, col_sides = sides_of(nrow), sides_of(ncol)
    log_a = log_a.reshape(-1, LANES)
    log_b = log_b.reshape(-1, LANES)
    rel, points, half_tgt, table = first_pass(sources, targets, block_cols.T, block_count.T)
    g_pot = -half_tgt
    f_pot = half_src = f_out = None
    for step in range(ITERS):
        if step > 0:
            rel = later_pass("row_pass", ROW_BIAS, True, points, g_pot, f_pot, table)
            f_pot = exchange("col", col_sides, 2 * step, rel, f_pot, log_a)
        else:
            f_pot, half_src = exchange("col", col_sides, 2 * step, rel, None, log_a, points)
        if step < ITERS - 1:
            rel = later_pass("col_pass", COL_BIAS, False, points, f_pot, g_pot, table)
        else:
            rel, f_out = later_pass("last_pass", COL_BIAS, False, points, f_pot, g_pot, table, half_src)
        g_pot = exchange("row", row_sides, 2 * step + 1, rel, g_pot, log_b)
    return (f_out.reshape(-1), (g_pot + half_tgt).reshape(-1))


def solution(mesh):
    return jax.shard_map(
        functools.partial(per_device, mesh.shape["row"], mesh.shape["col"]),
        mesh=mesh,
        in_specs=(
            P(None, "row"),
            P(None, "col"),
            P("row"),
            P("col"),
            P("row", "col"),
            P("row", "col"),
        ),
        out_specs=(P("row"), P("col")),
        check_vma=False,
    )
```

```python
import functools

import jax
import jax.numpy as jnp
from jax import lax
from jax.experimental import pallas as pl
from jax.experimental.pallas import tpu as pltpu
from jax.sharding import PartitionSpec as P

BLOCK = 256
LANES = 128
ITERS = 2
EPS = 0.05
LOG2_SCALE = 20.0 * 1.4426950408889634
NEG = -1e30
BIG_GROUP = 48
FIRST_GROUP = 24
SMALL_GROUP = 8
PAD = 16
CHUNKS = 4
SOURCE_CHUNKS = 8
ROW_SHIFT = 16
THRESHOLD = 2.0**-90
CEILING = 2.0**120
FIRST_BIAS = 40.0
ROW_BIAS = 112.0
COL_BIAS = 104.0
MESH = pl.DeviceIdType.MESH
MIB = 1024 * 1024


TABLE_START = 8


def add_pairs(cols_ref, count_ref, table, b, n, slots):
    for s in range(slots):
        table[TABLE_START + n + s] = (b << ROW_SHIFT) + cols_ref[s, b]
    return n + count_ref[0, b]


def close_table(table, total):
    for k in range(PAD):
        table[TABLE_START + total + k] = jnp.int32(-1)
    table[0] = total


def split3(v):
    hi = v.astype(jnp.bfloat16).astype(jnp.float32)
    rest = v - hi
    mid = rest.astype(jnp.bfloat16).astype(jnp.float32)
    return hi, mid, rest - mid


def half_norm(points, first, out_ref, b):
    blk = points[:, pl.ds(pl.multiple_of((first + b) * BLOCK, BLOCK), BLOCK)].astype(jnp.float32)
    norm = 0.5 * jnp.sum(blk * blk, 0, keepdims=True)
    out_ref[pl.ds(2 * b, 1), :] = norm[:, :LANES]
    out_ref[pl.ds(2 * b + 1, 1), :] = norm[:, LANES:]


def half_norms(points, first, out_ref, blocks):
    def one(b, carry):
        half_norm(points, first, out_ref, b)
        return carry

    lax.fori_loop(0, blocks, one, 0, unroll=4)


def lse_pass(
    bias, by_row, points, pot_red, pot_keep, table,
    rel_ref, red_parts, keep_parts, acc, top, touched, big=BIG_GROUP, arrive=None,
):
    nkeep = rel_ref.shape[0] // 2
    npairs = table[0]
    nred = pot_red.shape[0] // 2
    red_first, keep_first = (nkeep, 0) if by_row else (0, nred)
    shift = bias / LOG2_SCALE
    for part, value in enumerate(split3(pot_red[...])):
        red_parts[part] = value
    kept = pot_keep[...] + shift if pot_keep is not None else jnp.full(rel_ref.shape, shift, jnp.float32)
    for part, value in enumerate(split3(kept)):
        keep_parts[part] = value
    acc[...] = jnp.zeros_like(acc)
    touched[...] = jnp.zeros_like(touched)
    line = lax.broadcasted_iota(jnp.int32, (8, LANES), 0)
    zeros = jnp.zeros((8, LANES), jnp.float32)

    def rows(parts, index, first, ones):
        halves = []
        for half in range(2):
            out = jnp.where((line >= ones) & (line < ones + 3), 1.0, 0.0)
            for part in range(3):
                out = jnp.where(line == first + part, parts[part, pl.ds(2 * index + half, 1), :], out)
            halves.append(jnp.concatenate([out, zeros], 0).astype(jnp.bfloat16))
        return jnp.concatenate(halves, 1)

    def scores(p):
        word = table[TABLE_START + p]
        pair = jnp.maximum(word, 0)
        row, col = pair >> ROW_SHIFT, pair & ((1 << ROW_SHIFT) - 1)
        k, r = (row, col) if by_row else (col, row)
        into = jnp.where(word < 0, nkeep, k)
        rblk = points[:, pl.ds(pl.multiple_of((red_first + r) * BLOCK, BLOCK), BLOCK)]
        kblk = points[:, pl.ds(pl.multiple_of((keep_first + k) * BLOCK, BLOCK), BLOCK)]
        lhs = jnp.concatenate([rblk, rows(red_parts, r, 0, 3)], 0)
        rhs = jnp.concatenate([kblk, rows(keep_parts, k, 3, 0)], 0)
        z = lax.dot_general(lhs, rhs, (((0,), (0,)), ((), ())), preferred_element_type=jnp.float32)
        return z, into

    def add_pair(p, shifted):
        z, into = scores(p)
        if shifted:
            z = z - jnp.concatenate([top[pl.ds(2 * into + half, 1), :] for half in range(2)], 1)
        part = jnp.sum(jnp.exp2(z * LOG2_SCALE), 0, keepdims=True)
        acc[pl.ds(2 * into, 1), :] += part[:, :LANES]
        acc[pl.ds(2 * into + 1, 1), :] += part[:, LANES:]
        touched[pl.ds(2 * into, 2), :] = jnp.ones((2, LANES), jnp.float32)

    def groups(size, base, trips, here):
        def group(t, here):
            first = base + t * size
            if arrive is not None:
                last = table[TABLE_START + jnp.minimum(first + size, npairs) - 1]
                here = arrive(here, last >> ROW_SHIFT)
            for u in range(size):
                add_pair(first + u, False)
            return here

        return lax.fori_loop(0, trips, group, here)

    whole = (npairs + PAD - 1) // big
    left = jnp.maximum(npairs - whole * big, 0)
    here = groups(big, 0, whole, jnp.int32(0))
    here = groups(SMALL_GROUP, whole * big, (left + SMALL_GROUP - 1) // SMALL_GROUP, here)
    if arrive is not None:
        arrive(here, None)
    total = acc[: 2 * nkeep]
    live = touched[: 2 * nkeep] > 0.0
    rel_ref[...] = jnp.where(live, jnp.log2(total) - bias, NEG)
    fine = (total >= THRESHOLD) & (total <= CEILING)
    weak = jnp.max(jnp.where(live & ~fine, 1.0, 0.0))

    @pl.when(weak > 0.0)
    def _():
        top[...] = jnp.full_like(top, NEG)

        def top_pair(p, carry):
            z, into = scores(p)
            part = jnp.max(z, 0, keepdims=True)
            for half in range(2):
                at = pl.ds(2 * into + half, 1)
                top[at, :] = jnp.maximum(top[at, :], part[:, half * LANES : (half + 1) * LANES])
            return carry

        lax.fori_loop(0, npairs, top_pair, 0)
        acc[...] = jnp.zeros_like(acc)

        def sum_pair(p, carry):
            add_pair(p, True)
            return carry

        lax.fori_loop(0, npairs, sum_pair, 0)
        fixed = jnp.log2(acc[: 2 * nkeep]) + (top[: 2 * nkeep] * LOG2_SCALE - bias)
        rel_ref[...] = jnp.where(touched[: 2 * nkeep] > 0.0, fixed, NEG)


def first_kernel(
    slots, sources, targets, cols, counts,
    rel, points, half_tgt, table,
    pot_tgt, cols_here, counts_here, sem_src, sem_tgt, sem_list, *scratch,
):
    row_blocks = rel.shape[0] // 2
    col_blocks = half_tgt.shape[0] // 2

    def chunk(whole, first, sem, chunks, c):
        width = whole.shape[1] // chunks
        start = c * width if isinstance(c, int) else pl.multiple_of(c * width, LANES)
        into = pl.ds(first * BLOCK + start, width)
        return pltpu.make_async_copy(whole.at[:, pl.ds(start, width)], points.at[:, into], sem.at[c])

    list_copies = [
        pltpu.make_async_copy(cols, cols_here, sem_list.at[0]),
        pltpu.make_async_copy(counts, counts_here, sem_list.at[1]),
    ]
    tgt_copies = [chunk(targets, row_blocks, sem_tgt, CHUNKS, c) for c in range(CHUNKS)]
    src_copies = [chunk(sources, 0, sem_src, SOURCE_CHUNKS, c) for c in range(SOURCE_CHUNKS)]
    ahead = SOURCE_CHUNKS // CHUNKS
    for copy in list_copies + tgt_copies + src_copies[:ahead]:
        copy.start()
    for copy in list_copies:
        copy.wait()

    parts = col_blocks // 4
    per_part = row_blocks // parts

    def prepare(t, n):
        for u in range(4):
            half_norm(points, row_blocks, half_tgt, 4 * t + u)
        for u in range(per_part):
            n = add_pairs(cols_here, counts_here, table, per_part * t + u, n, slots)
        return n

    total = jnp.int32(0)
    for c, copy in enumerate(tgt_copies):
        copy.wait()
        for later in src_copies[(c + 1) * ahead : (c + 2) * ahead]:
            later.start()
        total = lax.fori_loop(c * parts // CHUNKS, (c + 1) * parts // CHUNKS, prepare, total)
    close_table(table, total)
    pot_tgt[...] = -half_tgt[...]

    def arrive(here, row):
        stop = SOURCE_CHUNKS if row is None else row // (row_blocks // SOURCE_CHUNKS) + 1

        def one(c, carry):
            chunk(sources, 0, sem_src, SOURCE_CHUNKS, c).wait()
            return carry

        lax.fori_loop(here, stop, one, 0)
        return jnp.maximum(here, stop)

    lse_pass(FIRST_BIAS, True, points, pot_tgt, None, table, rel, *scratch, big=FIRST_GROUP, arrive=arrive)


def last_kernel(bias, points, f_pot, g_pot, half_src, table, rel, f_final, f_here, sem, *scratch):
    f_here[...] = f_pot[...] + half_src[...]
    copy = pltpu.make_async_copy(f_here, f_final, sem)
    copy.start()
    lse_pass(bias, False, points, f_pot, g_pot, table, rel, *scratch)
    copy.wait()


VMEM = pl.BlockSpec(memory_space=pltpu.VMEM)
SMEM = pl.BlockSpec(memory_space=pltpu.SMEM)
HBM = pl.BlockSpec(memory_space=pltpu.HBM)
ANY = pl.BlockSpec(memory_space=pl.ANY)


def pass_scratch(nred, nkeep):
    return [
        pltpu.VMEM((3, 2 * nred, LANES), jnp.float32),
        pltpu.VMEM((3, 2 * nkeep, LANES), jnp.float32),
        pltpu.VMEM((2 * nkeep + 8, LANES), jnp.float32),
        pltpu.VMEM((2 * nkeep + 8, LANES), jnp.float32),
        pltpu.VMEM((2 * nkeep + 8, LANES), jnp.float32),
    ]


def potential(blocks):
    return jax.ShapeDtypeStruct((2 * blocks, LANES), jnp.float32)


def first_pass(sources, targets, cols, counts):
    slots = cols.shape[0]
    nkeep = sources.shape[1] // BLOCK
    nred = targets.shape[1] // BLOCK
    return pl.pallas_call(
        functools.partial(first_kernel, slots),
        out_shape=(
            potential(nkeep),
            jax.ShapeDtypeStruct((sources.shape[0], sources.shape[1] + targets.shape[1]), sources.dtype),
            potential(nred),
            jax.ShapeDtypeStruct((TABLE_START + nkeep * slots + PAD,), jnp.int32),
        ),
        in_specs=[HBM, HBM, HBM, HBM],
        out_specs=(VMEM, VMEM, VMEM, SMEM),
        scratch_shapes=[
            pltpu.VMEM((2 * nred, LANES), jnp.float32),
            pltpu.SMEM(cols.shape, jnp.int32),
            pltpu.SMEM(counts.shape, jnp.int32),
            pltpu.SemaphoreType.DMA((SOURCE_CHUNKS,)),
            pltpu.SemaphoreType.DMA((CHUNKS,)),
            pltpu.SemaphoreType.DMA((2,)),
        ]
        + pass_scratch(nred, nkeep),
        compiler_params=pltpu.CompilerParams(vmem_limit_bytes=24 * MIB),
        name="first_pass",
    )(*(pltpu.with_memory_space_constraint(a, pltpu.HBM) for a in (sources, targets, cols, counts)))


def later_pass(name, bias, by_row, points, pot_red, pot_keep, table, norms=None):
    nred, nkeep = pot_red.shape[0] // 2, pot_keep.shape[0] // 2
    params = pltpu.CompilerParams(vmem_limit_bytes=16 * MIB)
    if norms is None:
        return pl.pallas_call(
            functools.partial(lse_pass, bias, by_row),
            out_shape=potential(nkeep),
            in_specs=[VMEM] * 3 + [SMEM],
            out_specs=VMEM,
            scratch_shapes=pass_scratch(nred, nkeep),
            compiler_params=params,
            name=name,
        )(points, pot_red, pot_keep, table)
    return pl.pallas_call(
        functools.partial(last_kernel, bias),
        out_shape=(potential(nkeep), potential(nred)),
        in_specs=[VMEM] * 4 + [SMEM],
        out_specs=(VMEM, HBM),
        scratch_shapes=[pltpu.VMEM((2 * nred, LANES), jnp.float32), pltpu.SemaphoreType.DMA]
        + pass_scratch(nred, nkeep),
        compiler_params=params,
        name=name,
    )(points, pot_red, pot_keep, norms, table)


def offsets(outer, inner):
    def far(step):
        return min(step[0], outer - step[0]) + min(step[1], inner - step[1])

    steps = [(a, b) for a in range(outer) for b in range(inner) if a or b]
    return sorted(steps, key=lambda step: -far(step))


def exchange_kernel(axis, sides, has_old, with_norms, *refs):
    refs = list(refs)
    rel = refs.pop(0)
    old = refs.pop(0) if has_old else None
    logw = refs.pop(0)
    points = refs.pop(0) if with_norms else None
    out = refs.pop(0)
    norms = refs.pop(0) if with_norms else None
    landing, weights, wsem, send1, recv1, send2, recv2 = refs
    outer, inner = sides
    n = outer * inner
    steps = offsets(outer, inner)
    me = lax.axis_index(axis)
    peers = [
        lax.rem(me // inner + a, outer) * inner + lax.rem(lax.rem(me, inner) + b, inner) for a, b in steps
    ]
    chunk = rel.shape[0] // n
    mine = pl.ds(pl.multiple_of(me * chunk, 8), chunk)
    fetch = pltpu.make_async_copy(logw.at[mine], weights, wsem)
    fetch.start()

    barrier = pltpu.get_barrier_semaphore()
    for peer in peers:
        pl.semaphore_signal(barrier, inc=1, device_id={axis: peer}, device_id_type=MESH)
    pl.semaphore_wait(barrier, n - 1)

    def scatter(k):
        peer = peers[k]
        return pltpu.make_async_remote_copy(
            src_ref=rel.at[pl.ds(pl.multiple_of(peer * chunk, 8), chunk)],
            dst_ref=landing.at[k],
            send_sem=send1.at[k],
            recv_sem=recv1.at[k],
            device_id={axis: peer},
            device_id_type=MESH,
        )

    def gather(k):
        peer = peers[k]
        return pltpu.make_async_remote_copy(
            src_ref=out.at[mine],
            dst_ref=out.at[mine],
            send_sem=send2.at[k],
            recv_sem=recv2.at[k],
            device_id={axis: peer},
            device_id_type=MESH,
        )

    first = [scatter(k) for k in range(n - 1)]
    for copy in first:
        copy.start()
    if with_norms:
        half_norms(points, 0, norms, rel.shape[0] // 2)
    own = rel[mine]
    fetch.wait()
    base = EPS * weights[...]
    if has_old:
        base = base + old[mine]
    for copy in first:
        copy.wait_recv()
    top = jnp.maximum(own, jnp.max(landing[...], 0))
    total = jnp.exp2(own - top) + jnp.sum(jnp.exp2(landing[...] - top[None]), 0)
    out[mine] = base - (top + jnp.log2(total)) * (1.0 / LOG2_SCALE)
    second = [gather(k) for k in range(n - 1)]
    for copy in second:
        copy.start()
    for copy in second:
        copy.wait_recv()
    for copy in first:
        copy.wait_send()
    for copy in second:
        copy.wait_send()


def paired_exchange_kernel(axis, outer, rel, old, logw, out, landing, chips, weights, wsem, pair_sems, chip_send, chip_recv):
    me = lax.axis_index(axis)
    chip, core = me // 2, lax.rem(me, 2)
    half = rel.shape[0] // 2
    sibling = chip * 2 + 1 - core
    peers = [lax.rem(chip + a, outer) * 2 + core for a, _ in offsets(outer, 1)]
    mine = pl.ds(pl.multiple_of(core * half, 8), half)
    other = pl.ds(pl.multiple_of((1 - core) * half, 8), half)
    fetch = pltpu.make_async_copy(logw.at[mine], weights, wsem)
    fetch.start()

    barrier = pltpu.get_barrier_semaphore()
    for peer in peers + [sibling]:
        pl.semaphore_signal(barrier, inc=1, device_id={axis: peer}, device_id_type=MESH)
    pl.semaphore_wait(barrier, outer)

    def to(peer, src, dst, send, recv):
        return pltpu.make_async_remote_copy(
            src_ref=src, dst_ref=dst, send_sem=send, recv_sem=recv, device_id={axis: peer}, device_id_type=MESH
        )

    split = to(sibling, rel.at[other], landing, pair_sems.at[0], pair_sems.at[1])
    split.start()
    own = rel[mine]
    split.wait_recv()
    top = jnp.maximum(own, landing[...])
    chips[chip] = top + jnp.log2(jnp.exp2(own - top) + jnp.exp2(landing[...] - top))
    spread = [
        to(peer, chips.at[chip], chips.at[chip], chip_send.at[k], chip_recv.at[k]) for k, peer in enumerate(peers)
    ]
    for copy in spread:
        copy.start()
    fetch.wait()
    base = old[mine] + EPS * weights[...]
    for copy in spread:
        copy.wait_recv()
    parts = [chips[c] for c in range(outer)]
    top = functools.reduce(jnp.maximum, parts)
    total = functools.reduce(jnp.add, [jnp.exp2(part - top) for part in parts])
    out[mine] = base - (top + jnp.log2(total)) * (1.0 / LOG2_SCALE)
    join = to(sibling, out.at[mine], out.at[mine], pair_sems.at[2], pair_sems.at[3])
    join.start()
    join.wait_recv()
    for copy in [split, join] + spread:
        copy.wait_send()


def paired_exchange(axis, outer, ident, rel, old, logw):
    lines = rel.shape[0]
    half = (lines // 2, LANES)
    return pl.pallas_call(
        functools.partial(paired_exchange_kernel, axis, outer),
        out_shape=jax.ShapeDtypeStruct((lines, LANES), jnp.float32),
        in_specs=[VMEM, VMEM, ANY],
        out_specs=VMEM,
        scratch_shapes=[
            pltpu.VMEM(half, jnp.float32),
            pltpu.VMEM((outer,) + half, jnp.float32),
            pltpu.VMEM(half, jnp.float32),
            pltpu.SemaphoreType.DMA,
            pltpu.SemaphoreType.DMA((4,)),
            pltpu.SemaphoreType.DMA((outer - 1,)),
            pltpu.SemaphoreType.DMA((outer - 1,)),
        ],
        compiler_params=pltpu.CompilerParams(
            collective_id=ident, has_side_effects=True, vmem_limit_bytes=4 * MIB
        ),
        name=f"exchange_{axis}_{ident}",
    )(rel, old, logw)


def exchange(axis, sides, ident, rel, old, logw, points=None):
    lines = rel.shape[0]
    n = sides[0] * sides[1]
    shape = jax.ShapeDtypeStruct((lines, LANES), jnp.float32)
    has_old, with_norms = old is not None, points is not None
    args = [rel] + ([old] if has_old else []) + [logw] + ([points] if with_norms else [])
    specs = [VMEM] + ([VMEM] if has_old else []) + [ANY] + ([VMEM] if with_norms else [])
    return pl.pallas_call(
        functools.partial(exchange_kernel, axis, sides, has_old, with_norms),
        out_shape=(shape, shape) if with_norms else shape,
        in_specs=specs,
        out_specs=(VMEM, VMEM) if with_norms else VMEM,
        scratch_shapes=[
            pltpu.VMEM((n - 1, lines // n, LANES), jnp.float32),
            pltpu.VMEM((lines // n, LANES), jnp.float32),
            pltpu.SemaphoreType.DMA,
        ]
        + [pltpu.SemaphoreType.DMA((n - 1,))] * 4,
        compiler_params=pltpu.CompilerParams(
            collective_id=ident, has_side_effects=True, vmem_limit_bytes=(12 if with_norms else 4) * MIB
        ),
        name=f"exchange_{axis}_{ident}",
    )(*args)


def sides_of(n):
    return (4, n // 4) if n % 4 == 0 else (n, 1)


def per_device(nrow, ncol, sources, targets, log_a, log_b, block_cols, block_count):
    col_sides = sides_of(ncol)
    log_a = log_a.reshape(-1, LANES)
    log_b = log_b.reshape(-1, LANES)
    rel, points, half_tgt, table = first_pass(sources, targets, block_cols.T, block_count.T)
    g_pot = -half_tgt
    f_pot = half_src = f_out = None
    for step in range(ITERS):
        if step > 0:
            rel = later_pass("row_pass", ROW_BIAS, True, points, g_pot, f_pot, table)
            f_pot = exchange("col", col_sides, 2 * step, rel, f_pot, log_a)
        else:
            f_pot, half_src = exchange("col", col_sides, 2 * step, rel, None, log_a, points)
        if step < ITERS - 1:
            rel = later_pass("col_pass", COL_BIAS, False, points, f_pot, g_pot, table)
        else:
            rel, f_out = later_pass("last_pass", COL_BIAS, False, points, f_pot, g_pot, table, half_src)
        g_pot = paired_exchange("row", nrow // 2, 2 * step + 1, rel, g_pot, log_b)
    return (f_out.reshape(-1), (g_pot + half_tgt).reshape(-1))


def solution(mesh):
    return jax.shard_map(
        functools.partial(per_device, mesh.shape["row"], mesh.shape["col"]),
        mesh=mesh,
        in_specs=(
            P(None, "row"),
            P(None, "col"),
            P("row"),
            P("col"),
            P("row", "col"),
            P("row", "col"),
        ),
        out_specs=(P("row"), P("col")),
        check_vma=False,
    )
```

```python
import functools

import jax
import jax.numpy as jnp
from jax import lax
from jax.experimental import pallas as pl
from jax.experimental.pallas import tpu as pltpu
from jax.sharding import PartitionSpec as P

BLOCK = 256
LANES = 128
ITERS = 2
EPS = 0.05
LOG2_SCALE = 20.0 * 1.4426950408889634
NEG = -1e30
BIG_GROUP = 48
FIRST_GROUP = 24
SMALL_GROUP = 8
PAD = 16
CHUNKS = 4
SOURCE_CHUNKS = 8
ROW_SHIFT = 16
THRESHOLD = 2.0**-90
CEILING = 2.0**120
FIRST_BIAS = 40.0
ROW_BIAS = 112.0
COL_BIAS = 104.0
MESH = pl.DeviceIdType.MESH
MIB = 1024 * 1024


TABLE_START = 8


def add_pairs(cols_ref, count_ref, table, b, n, slots):
    for s in range(slots):
        table[TABLE_START + n + s] = (b << ROW_SHIFT) + cols_ref[s, b]
    return n + count_ref[0, b]


def close_table(table, total):
    for k in range(PAD):
        table[TABLE_START + total + k] = jnp.int32(-1)
    table[0] = total


def split3(v):
    hi = v.astype(jnp.bfloat16).astype(jnp.float32)
    rest = v - hi
    mid = rest.astype(jnp.bfloat16).astype(jnp.float32)
    return hi, mid, rest - mid


def half_norm(points, first, out_ref, b):
    blk = points[:, pl.ds(pl.multiple_of((first + b) * BLOCK, BLOCK), BLOCK)].astype(jnp.float32)
    norm = 0.5 * jnp.sum(blk * blk, 0, keepdims=True)
    out_ref[pl.ds(2 * b, 1), :] = norm[:, :LANES]
    out_ref[pl.ds(2 * b + 1, 1), :] = norm[:, LANES:]


def half_norms(points, first, out_ref, blocks):
    def one(b, carry):
        half_norm(points, first, out_ref, b)
        return carry

    lax.fori_loop(0, blocks, one, 0, unroll=4)


def lse_pass(
    bias, by_row, points, pot_red, pot_keep, table,
    rel_ref, red_parts, keep_parts, acc, top, touched, big=BIG_GROUP, arrive=None,
):
    nkeep = rel_ref.shape[0] // 2
    npairs = table[0]
    nred = pot_red.shape[0] // 2
    red_first, keep_first = (nkeep, 0) if by_row else (0, nred)
    shift = bias / LOG2_SCALE
    for part, value in enumerate(split3(pot_red[...])):
        red_parts[part] = value
    kept = pot_keep[...] + shift if pot_keep is not None else jnp.full(rel_ref.shape, shift, jnp.float32)
    for part, value in enumerate(split3(kept)):
        keep_parts[part] = value
    acc[...] = jnp.zeros_like(acc)
    touched[...] = jnp.zeros_like(touched)
    line = lax.broadcasted_iota(jnp.int32, (8, LANES), 0)
    zeros = jnp.zeros((8, LANES), jnp.float32)

    def rows(parts, index, first, ones):
        halves = []
        for half in range(2):
            out = jnp.where((line >= ones) & (line < ones + 3), 1.0, 0.0)
            for part in range(3):
                out = jnp.where(line == first + part, parts[part, pl.ds(2 * index + half, 1), :], out)
            halves.append(jnp.concatenate([out, zeros], 0).astype(jnp.bfloat16))
        return jnp.concatenate(halves, 1)

    def scores(p):
        word = table[TABLE_START + p]
        pair = jnp.maximum(word, 0)
        row, col = pair >> ROW_SHIFT, pair & ((1 << ROW_SHIFT) - 1)
        k, r = (row, col) if by_row else (col, row)
        into = jnp.where(word < 0, nkeep, k)
        rblk = points[:, pl.ds(pl.multiple_of((red_first + r) * BLOCK, BLOCK), BLOCK)]
        kblk = points[:, pl.ds(pl.multiple_of((keep_first + k) * BLOCK, BLOCK), BLOCK)]
        lhs = jnp.concatenate([rblk, rows(red_parts, r, 0, 3)], 0)
        rhs = jnp.concatenate([kblk, rows(keep_parts, k, 3, 0)], 0)
        z = lax.dot_general(lhs, rhs, (((0,), (0,)), ((), ())), preferred_element_type=jnp.float32)
        return z, into

    def add_pair(p, shifted):
        z, into = scores(p)
        if shifted:
            z = z - jnp.concatenate([top[pl.ds(2 * into + half, 1), :] for half in range(2)], 1)
        part = jnp.sum(jnp.exp2(z * LOG2_SCALE), 0, keepdims=True)
        acc[pl.ds(2 * into, 1), :] += part[:, :LANES]
        acc[pl.ds(2 * into + 1, 1), :] += part[:, LANES:]
        touched[pl.ds(2 * into, 2), :] = jnp.ones((2, LANES), jnp.float32)

    def groups(size, base, trips, here):
        def group(t, here):
            first = base + t * size
            if arrive is not None:
                last = table[TABLE_START + jnp.minimum(first + size, npairs) - 1]
                here = arrive(here, last >> ROW_SHIFT)
            for u in range(size):
                add_pair(first + u, False)
            return here

        return lax.fori_loop(0, trips, group, here)

    whole = (npairs + PAD - 1) // big
    left = jnp.maximum(npairs - whole * big, 0)
    here = groups(big, 0, whole, jnp.int32(0))
    here = groups(SMALL_GROUP, whole * big, (left + SMALL_GROUP - 1) // SMALL_GROUP, here)
    if arrive is not None:
        arrive(here, None)
    total = acc[: 2 * nkeep]
    live = touched[: 2 * nkeep] > 0.0
    rel_ref[...] = jnp.where(live, jnp.log2(total) - bias, NEG)
    fine = (total >= THRESHOLD) & (total <= CEILING)
    weak = jnp.max(jnp.where(live & ~fine, 1.0, 0.0))

    @pl.when(weak > 0.0)
    def _():
        top[...] = jnp.full_like(top, NEG)

        def top_pair(p, carry):
            z, into = scores(p)
            part = jnp.max(z, 0, keepdims=True)
            for half in range(2):
                at = pl.ds(2 * into + half, 1)
                top[at, :] = jnp.maximum(top[at, :], part[:, half * LANES : (half + 1) * LANES])
            return carry

        lax.fori_loop(0, npairs, top_pair, 0)
        acc[...] = jnp.zeros_like(acc)

        def sum_pair(p, carry):
            add_pair(p, True)
            return carry

        lax.fori_loop(0, npairs, sum_pair, 0)
        fixed = jnp.log2(acc[: 2 * nkeep]) + (top[: 2 * nkeep] * LOG2_SCALE - bias)
        rel_ref[...] = jnp.where(touched[: 2 * nkeep] > 0.0, fixed, NEG)


def first_kernel(
    slots, sources, targets, cols, counts,
    rel, points, half_tgt, table,
    pot_tgt, cols_here, counts_here, sem_src, sem_tgt, sem_list, *scratch,
):
    row_blocks = rel.shape[0] // 2
    col_blocks = half_tgt.shape[0] // 2

    def chunk(whole, first, sem, chunks, c):
        width = whole.shape[1] // chunks
        start = c * width if isinstance(c, int) else pl.multiple_of(c * width, LANES)
        into = pl.ds(first * BLOCK + start, width)
        return pltpu.make_async_copy(whole.at[:, pl.ds(start, width)], points.at[:, into], sem.at[c])

    list_copies = [
        pltpu.make_async_copy(cols, cols_here, sem_list.at[0]),
        pltpu.make_async_copy(counts, counts_here, sem_list.at[1]),
    ]
    tgt_copies = [chunk(targets, row_blocks, sem_tgt, CHUNKS, c) for c in range(CHUNKS)]
    src_copies = [chunk(sources, 0, sem_src, SOURCE_CHUNKS, c) for c in range(SOURCE_CHUNKS)]
    for copy in list_copies + tgt_copies + src_copies:
        copy.start()
    for copy in list_copies:
        copy.wait()

    parts = col_blocks // 4
    per_part = row_blocks // parts

    def prepare(t, n):
        for u in range(4):
            half_norm(points, row_blocks, half_tgt, 4 * t + u)
        for u in range(per_part):
            n = add_pairs(cols_here, counts_here, table, per_part * t + u, n, slots)
        return n

    total = jnp.int32(0)
    for c, copy in enumerate(tgt_copies):
        copy.wait()
        total = lax.fori_loop(c * parts // CHUNKS, (c + 1) * parts // CHUNKS, prepare, total)
    close_table(table, total)
    pot_tgt[...] = -half_tgt[...]

    def arrive(here, row):
        stop = SOURCE_CHUNKS if row is None else row // (row_blocks // SOURCE_CHUNKS) + 1

        def one(c, carry):
            chunk(sources, 0, sem_src, SOURCE_CHUNKS, c).wait()
            return carry

        lax.fori_loop(here, stop, one, 0)
        return jnp.maximum(here, stop)

    lse_pass(FIRST_BIAS, True, points, pot_tgt, None, table, rel, *scratch, big=FIRST_GROUP, arrive=arrive)


def last_kernel(bias, points, f_pot, g_pot, half_src, table, rel, f_final, f_here, sem, *scratch):
    f_here[...] = f_pot[...] + half_src[...]
    copy = pltpu.make_async_copy(f_here, f_final, sem)
    copy.start()
    lse_pass(bias, False, points, f_pot, g_pot, table, rel, *scratch)
    copy.wait()


VMEM = pl.BlockSpec(memory_space=pltpu.VMEM)
SMEM = pl.BlockSpec(memory_space=pltpu.SMEM)
HBM = pl.BlockSpec(memory_space=pltpu.HBM)
ANY = pl.BlockSpec(memory_space=pl.ANY)


def pass_scratch(nred, nkeep):
    return [
        pltpu.VMEM((3, 2 * nred, LANES), jnp.float32),
        pltpu.VMEM((3, 2 * nkeep, LANES), jnp.float32),
        pltpu.VMEM((2 * nkeep + 8, LANES), jnp.float32),
        pltpu.VMEM((2 * nkeep + 8, LANES), jnp.float32),
        pltpu.VMEM((2 * nkeep + 8, LANES), jnp.float32),
    ]


def potential(blocks):
    return jax.ShapeDtypeStruct((2 * blocks, LANES), jnp.float32)


def first_pass(sources, targets, cols, counts):
    slots = cols.shape[0]
    nkeep = sources.shape[1] // BLOCK
    nred = targets.shape[1] // BLOCK
    return pl.pallas_call(
        functools.partial(first_kernel, slots),
        out_shape=(
            potential(nkeep),
            jax.ShapeDtypeStruct((sources.shape[0], sources.shape[1] + targets.shape[1]), sources.dtype),
            potential(nred),
            jax.ShapeDtypeStruct((TABLE_START + nkeep * slots + PAD,), jnp.int32),
        ),
        in_specs=[HBM, HBM, HBM, HBM],
        out_specs=(VMEM, VMEM, VMEM, SMEM),
        scratch_shapes=[
            pltpu.VMEM((2 * nred, LANES), jnp.float32),
            pltpu.SMEM(cols.shape, jnp.int32),
            pltpu.SMEM(counts.shape, jnp.int32),
            pltpu.SemaphoreType.DMA((SOURCE_CHUNKS,)),
            pltpu.SemaphoreType.DMA((CHUNKS,)),
            pltpu.SemaphoreType.DMA((2,)),
        ]
        + pass_scratch(nred, nkeep),
        compiler_params=pltpu.CompilerParams(vmem_limit_bytes=24 * MIB),
        name="first_pass",
    )(*(pltpu.with_memory_space_constraint(a, pltpu.HBM) for a in (sources, targets, cols, counts)))


def later_pass(name, bias, by_row, points, pot_red, pot_keep, table, norms=None):
    nred, nkeep = pot_red.shape[0] // 2, pot_keep.shape[0] // 2
    params = pltpu.CompilerParams(vmem_limit_bytes=16 * MIB)
    if norms is None:
        return pl.pallas_call(
            functools.partial(lse_pass, bias, by_row),
            out_shape=potential(nkeep),
            in_specs=[VMEM] * 3 + [SMEM],
            out_specs=VMEM,
            scratch_shapes=pass_scratch(nred, nkeep),
            compiler_params=params,
            name=name,
        )(points, pot_red, pot_keep, table)
    return pl.pallas_call(
        functools.partial(last_kernel, bias),
        out_shape=(potential(nkeep), potential(nred)),
        in_specs=[VMEM] * 4 + [SMEM],
        out_specs=(VMEM, HBM),
        scratch_shapes=[pltpu.VMEM((2 * nred, LANES), jnp.float32), pltpu.SemaphoreType.DMA]
        + pass_scratch(nred, nkeep),
        compiler_params=params,
        name=name,
    )(points, pot_red, pot_keep, norms, table)


def offsets(outer, inner):
    def far(step):
        return min(step[0], outer - step[0]) + min(step[1], inner - step[1])

    steps = [(a, b) for a in range(outer) for b in range(inner) if a or b]
    return sorted(steps, key=lambda step: -far(step))


def exchange_kernel(axis, sides, has_old, with_norms, *refs):
    refs = list(refs)
    rel = refs.pop(0)
    old = refs.pop(0) if has_old else None
    logw = refs.pop(0)
    points = refs.pop(0) if with_norms else None
    out = refs.pop(0)
    norms = refs.pop(0) if with_norms else None
    landing, weights, wsem, send1, recv1, send2, recv2 = refs
    outer, inner = sides
    n = outer * inner
    steps = offsets(outer, inner)
    me = lax.axis_index(axis)
    peers = [
        lax.rem(me // inner + a, outer) * inner + lax.rem(lax.rem(me, inner) + b, inner) for a, b in steps
    ]
    chunk = rel.shape[0] // n
    mine = pl.ds(pl.multiple_of(me * chunk, 8), chunk)
    fetch = pltpu.make_async_copy(logw.at[mine], weights, wsem)
    fetch.start()

    barrier = pltpu.get_barrier_semaphore()
    for peer in peers:
        pl.semaphore_signal(barrier, inc=1, device_id={axis: peer}, device_id_type=MESH)
    pl.semaphore_wait(barrier, n - 1)

    def scatter(k):
        peer = peers[k]
        return pltpu.make_async_remote_copy(
            src_ref=rel.at[pl.ds(pl.multiple_of(peer * chunk, 8), chunk)],
            dst_ref=landing.at[k],
            send_sem=send1.at[k],
            recv_sem=recv1.at[k],
            device_id={axis: peer},
            device_id_type=MESH,
        )

    def gather(k):
        peer = peers[k]
        return pltpu.make_async_remote_copy(
            src_ref=out.at[mine],
            dst_ref=out.at[mine],
            send_sem=send2.at[k],
            recv_sem=recv2.at[k],
            device_id={axis: peer},
            device_id_type=MESH,
        )

    first = [scatter(k) for k in range(n - 1)]
    for copy in first:
        copy.start()
    if with_norms:
        half_norms(points, 0, norms, rel.shape[0] // 2)
    own = rel[mine]
    fetch.wait()
    base = EPS * weights[...]
    if has_old:
        base = base + old[mine]
    for copy in first:
        copy.wait_recv()
    top = jnp.maximum(own, jnp.max(landing[...], 0))
    total = jnp.exp2(own - top) + jnp.sum(jnp.exp2(landing[...] - top[None]), 0)
    out[mine] = base - (top + jnp.log2(total)) * (1.0 / LOG2_SCALE)
    second = [gather(k) for k in range(n - 1)]
    for copy in second:
        copy.start()
    for copy in second:
        copy.wait_recv()
    for copy in first:
        copy.wait_send()
    for copy in second:
        copy.wait_send()


def paired_exchange_kernel(axis, outer, rel, old, logw, out, landing, chips, weights, wsem, pair_sems, chip_send, chip_recv):
    me = lax.axis_index(axis)
    chip, core = me // 2, lax.rem(me, 2)
    half = rel.shape[0] // 2
    sibling = chip * 2 + 1 - core
    peers = [lax.rem(chip + a, outer) * 2 + core for a, _ in offsets(outer, 1)]
    mine = pl.ds(pl.multiple_of(core * half, 8), half)
    other = pl.ds(pl.multiple_of((1 - core) * half, 8), half)
    fetch = pltpu.make_async_copy(logw.at[mine], weights, wsem)
    fetch.start()

    barrier = pltpu.get_barrier_semaphore()
    for peer in peers + [sibling]:
        pl.semaphore_signal(barrier, inc=1, device_id={axis: peer}, device_id_type=MESH)
    pl.semaphore_wait(barrier, outer)

    def to(peer, src, dst, send, recv):
        return pltpu.make_async_remote_copy(
            src_ref=src, dst_ref=dst, send_sem=send, recv_sem=recv, device_id={axis: peer}, device_id_type=MESH
        )

    split = to(sibling, rel.at[other], landing, pair_sems.at[0], pair_sems.at[1])
    split.start()
    own = rel[mine]
    split.wait_recv()
    top = jnp.maximum(own, landing[...])
    chips[chip] = top + jnp.log2(jnp.exp2(own - top) + jnp.exp2(landing[...] - top))
    spread = [
        to(peer, chips.at[chip], chips.at[chip], chip_send.at[k], chip_recv.at[k]) for k, peer in enumerate(peers)
    ]
    for copy in spread:
        copy.start()
    fetch.wait()
    base = old[mine] + EPS * weights[...]
    for copy in spread:
        copy.wait_recv()
    parts = [chips[c] for c in range(outer)]
    top = functools.reduce(jnp.maximum, parts)
    total = functools.reduce(jnp.add, [jnp.exp2(part - top) for part in parts])
    out[mine] = base - (top + jnp.log2(total)) * (1.0 / LOG2_SCALE)
    join = to(sibling, out.at[mine], out.at[mine], pair_sems.at[2], pair_sems.at[3])
    join.start()
    join.wait_recv()
    for copy in [split, join] + spread:
        copy.wait_send()


def paired_exchange(axis, outer, ident, rel, old, logw):
    lines = rel.shape[0]
    half = (lines // 2, LANES)
    return pl.pallas_call(
        functools.partial(paired_exchange_kernel, axis, outer),
        out_shape=jax.ShapeDtypeStruct((lines, LANES), jnp.float32),
        in_specs=[VMEM, VMEM, ANY],
        out_specs=VMEM,
        scratch_shapes=[
            pltpu.VMEM(half, jnp.float32),
            pltpu.VMEM((outer,) + half, jnp.float32),
            pltpu.VMEM(half, jnp.float32),
            pltpu.SemaphoreType.DMA,
            pltpu.SemaphoreType.DMA((4,)),
            pltpu.SemaphoreType.DMA((outer - 1,)),
            pltpu.SemaphoreType.DMA((outer - 1,)),
        ],
        compiler_params=pltpu.CompilerParams(
            collective_id=ident, has_side_effects=True, vmem_limit_bytes=4 * MIB
        ),
        name=f"exchange_{axis}_{ident}",
    )(rel, old, logw)


def exchange(axis, sides, ident, rel, old, logw, points=None):
    lines = rel.shape[0]
    n = sides[0] * sides[1]
    shape = jax.ShapeDtypeStruct((lines, LANES), jnp.float32)
    has_old, with_norms = old is not None, points is not None
    args = [rel] + ([old] if has_old else []) + [logw] + ([points] if with_norms else [])
    specs = [VMEM] + ([VMEM] if has_old else []) + [ANY] + ([VMEM] if with_norms else [])
    return pl.pallas_call(
        functools.partial(exchange_kernel, axis, sides, has_old, with_norms),
        out_shape=(shape, shape) if with_norms else shape,
        in_specs=specs,
        out_specs=(VMEM, VMEM) if with_norms else VMEM,
        scratch_shapes=[
            pltpu.VMEM((n - 1, lines // n, LANES), jnp.float32),
            pltpu.VMEM((lines // n, LANES), jnp.float32),
            pltpu.SemaphoreType.DMA,
        ]
        + [pltpu.SemaphoreType.DMA((n - 1,))] * 4,
        compiler_params=pltpu.CompilerParams(
            collective_id=ident, has_side_effects=True, vmem_limit_bytes=(12 if with_norms else 4) * MIB
        ),
        name=f"exchange_{axis}_{ident}",
    )(*args)


def sides_of(n):
    return (4, n // 4) if n % 4 == 0 else (n, 1)


def per_device(nrow, ncol, sources, targets, log_a, log_b, block_cols, block_count):
    col_sides = sides_of(ncol)
    log_a = log_a.reshape(-1, LANES)
    log_b = log_b.reshape(-1, LANES)
    rel, points, half_tgt, table = first_pass(sources, targets, block_cols.T, block_count.T)
    g_pot = -half_tgt
    f_pot = half_src = f_out = None
    for step in range(ITERS):
        if step > 0:
            rel = later_pass("row_pass", ROW_BIAS, True, points, g_pot, f_pot, table)
            f_pot = exchange("col", col_sides, 2 * step, rel, f_pot, log_a)
        else:
            f_pot, half_src = exchange("col", col_sides, 2 * step, rel, None, log_a, points)
        if step < ITERS - 1:
            rel = later_pass("col_pass", COL_BIAS, False, points, f_pot, g_pot, table)
        else:
            rel, f_out = later_pass("last_pass", COL_BIAS, False, points, f_pot, g_pot, table, half_src)
        g_pot = paired_exchange("row", nrow // 2, 2 * step + 1, rel, g_pot, log_b)
    return (f_out.reshape(-1), (g_pot + half_tgt).reshape(-1))


def solution(mesh):
    return jax.shard_map(
        functools.partial(per_device, mesh.shape["row"], mesh.shape["col"]),
        mesh=mesh,
        in_specs=(
            P(None, "row"),
            P(None, "col"),
            P("row"),
            P("col"),
            P("row", "col"),
            P("row", "col"),
        ),
        out_specs=(P("row"), P("col")),
        check_vma=False,
    )
```
